512 devices in a mesh: section: 16 (over z_lo, x), feat: 32 (over y, z_hi, core).
Axes of the slice: x: 4, y: 8, z: 8 (z_hi: 2, z_lo: 4; z = z_hi * 4 + z_lo), core: 2. Of those that a mesh axis runs over, the one named last changes fastest.
Arguments:
- decoders: bfloat16 [16, 4096, 4608], P('section', 'feat'), may hold values from -0.09375 to 0.09375
- encoders: bfloat16 [16, 4096, 4608], P('section', 'feat'), may hold values from -6 to 6
- out_proj: bfloat16 [16, 4096, 4608], P('section', 'feat'), may hold values from -0.09375 to 0.09375
- value_proj: bfloat16 [16, 4608, 4096], P('section', None, 'feat'), may hold values from -0.09375 to 0.09375
- attention: float32 [16, 32, 16, 16], P('section', 'feat'), may hold values from 0 to 1, as said below
- norm_scale: float32 [16, 16], P('section'), may hold values from 0.05 to 0.5
- act_ids: int32 [16, 4096], P('section'), may hold values from 0 to 4095, as said below
- act_values: float32 [16, 4096], P('section', 'feat'), may hold values from 0.1 to 10
- target_ids: int32 [64], P('section'), may hold values from 0 to 4095
- target_pos: int32 [64], P('section'), may hold values from 0 to 15
Outputs:
- edges: float32 [16, 64, 4096], P('section', None, 'feat')
The draws below stay inside these ranges and needn't reach their ends.
Inputs may be any that keep to these rules, and one draw needn't show every extreme that they name: Every row attention[l, h, p, :] is nonnegative, zero at keys after p, and sums to one. `act_ids`: A feature id f is held by shard f // 128 of feat. In each aligned block of 128 entries of a layer (the entries of one device), at most 8 ids lie in one shard, and in every block some shard has exactly 8.
All inputs are finite; a program needn't handle non-finite values.
Results may differ from the reference program's by a relative error of at most 0.015.
Values may be sent and summed in bfloat16 or wider, within the bound.
No kernel may reach another device: no remote copies, remote signals or barrier semaphores. Data moves between devices by JAX's collectives and lax.ppermute only.
A program may use at most 64 MiB of HBM per device.

```python
import math
import jax
import jax.numpy as jnp
from jax import lax

D = 4608
HD = 128
SEQ = 16
FEAT_DEV = 128
TB = 4
K_ACT = 256
HEADS = 32
LAYERS = 16
TARGETS = 64
ENTRIES = 4096
FEATS = 4096
AE = 128
CAP = 8
N_FEAT = 32


def draw_attention(key, part):
    weights = jax.random.uniform(key, (LAYERS, HEADS, SEQ, SEQ), jnp.float32, 0.05, 1.0)
    query_index = lax.broadcasted_iota(jnp.int32, (SEQ, SEQ), 0)
    key_index = lax.broadcasted_iota(jnp.int32, (SEQ, SEQ), 1)
    weights = jnp.where(query_index >= key_index, weights, 0.0)
    return weights / jnp.sum(weights, axis=3, keepdims=True)


def draw_act_ids(key, part):
    slot_total = N_FEAT * CAP
    key_list = jax.random.split(jax.random.fold_in(key, 11), 4)
    levels = jax.random.randint(key_list[0], (LAYERS, N_FEAT), 0, 4)
    offsets = jax.random.randint(key_list[1], (LAYERS, 1), 0, N_FEAT)
    slot_noise = jax.random.randint(key_list[2], (LAYERS, N_FEAT, slot_total), 0, 4096)
    locals_drawn = jax.random.randint(key_list[3], (LAYERS, N_FEAT, slot_total), 0, FEAT_DEV)
    slot_iota = jnp.arange(slot_total, dtype=jnp.int32)
    slot_owner = slot_iota // CAP
    forced = (jnp.arange(N_FEAT, dtype=jnp.int32)[None, :] + offsets) % N_FEAT
    slot_level = jnp.repeat(levels, CAP, axis=1)[:, None, :]
    slot_score = slot_level * (1024 * slot_total) + slot_noise * slot_total + slot_iota[None, None, :]
    is_forced = slot_owner[None, None, :] == forced[:, :, None]
    slot_score = jnp.where(is_forced, slot_iota[None, None, :] - slot_total, slot_score)
    chosen = jnp.argsort(slot_score, axis=2)[:, :, :AE]
    first_slot = forced[:, :, None] * CAP
    local_slot = jnp.where(slot_iota[None, None, :] == first_slot, FEAT_DEV - 1, jnp.where(slot_iota[None, None, :] == first_slot + 1, 0, locals_drawn))
    local_ids = jnp.take_along_axis(local_slot, chosen, axis=2)
    feature_ids = chosen // CAP * FEAT_DEV + local_ids
    return feature_ids.reshape(LAYERS, N_FEAT * AE).astype(jnp.int32)


def plant(values, own_key, smallest, high):
    index_at = [jax.random.randint(jax.random.fold_in(own_key, axis), (), 0, length) for axis, length in enumerate(values.shape)]
    main_axis = values.shape.index(max(values.shape))
    neighbour = index_at[:main_axis] + [(index_at[main_axis] + 1) % values.shape[main_axis]] + index_at[main_axis + 1:]
    return values.at[tuple(index_at)].set(smallest).at[tuple(neighbour)].set(high)


def level_of(stream_key, dims, pieces, smallest, high):
    factor_of = 1.0
    for position, blocks in pieces:
        heights = jax.random.uniform(jax.random.fold_in(jax.random.fold_in(stream_key, 6), position), (blocks,), jnp.float32, smallest / len(pieces), high / len(pieces))
        factor_of = factor_of * jnp.repeat(jnp.exp(heights), dims[position] // blocks).reshape((-1,) + (1,) * (len(dims) - 1 - position))
    return factor_of


def normal_values(rng, shape, deviation, limit, shards=(), kind=jnp.bfloat16):
    loudness = level_of(rng, shape, shards, -0.22, 0.18) if shards else 1.0
    entries = jax.random.normal(rng, shape, jnp.float32) * deviation * loudness
    return jnp.minimum(jnp.maximum(entries, -limit), limit).astype(kind)


def setup_inputs(seed: int = 0) -> dict:
    streams_of = jax.random.split(jax.random.key(seed), 11)
    return {
        "decoders": normal_values(streams_of[0], (LAYERS, FEATS, D), D ** -0.5, 0.09375, ((0, 16), (1, 32))),
        "encoders": normal_values(streams_of[1], (LAYERS, FEATS, D), 1.0, 6.0, ((0, 16), (1, 32))),
        "out_proj": normal_values(streams_of[2], (LAYERS, HEADS * HD, D), (HEADS * HD) ** -0.5, 0.09375, ((0, 16), (1, 32))),
        "value_proj": normal_values(streams_of[3], (LAYERS, D, HEADS * HD), D ** -0.5, 0.09375, ((0, 16), (2, 32))),
        "attention": draw_attention(jax.random.fold_in(streams_of[10], 71), 0),
        "norm_scale": jnp.clip(jnp.exp(math.log(0.5) - 2.3025851 * jax.random.uniform(streams_of[5], (LAYERS, SEQ), jnp.float32) ** level_of(streams_of[5], (LAYERS, SEQ), ((0, 16),), -0.2, 0.2)), 0.05, 0.5),
        "act_ids": draw_act_ids(jax.random.fold_in(streams_of[10], 71), 0),
        "act_values": jnp.clip(jnp.exp(math.log(10.0) - 4.6051702 * jax.random.uniform(streams_of[7], (LAYERS, ENTRIES), jnp.float32) ** level_of(streams_of[7], (LAYERS, ENTRIES), ((0, 16), (1, 32)), -0.2, 0.2)), 0.1, 10.0),
        "target_ids": plant(jax.random.randint(streams_of[8], (TARGETS,), 0, FEATS), jax.random.fold_in(streams_of[8], 1), 0, FEATS - 1).astype(jnp.int32),
        "target_pos": plant(jax.random.randint(streams_of[9], (TARGETS,), 0, SEQ), jax.random.fold_in(streams_of[9], 1), 0, SEQ - 1).astype(jnp.int32),
    }


def reference(decoders, encoders, out_proj, value_proj, attention, norm_scale, act_ids, act_values, target_ids, target_pos):
    positions = jnp.arange(SEQ, dtype=jnp.int32)
    entry_pos = jnp.arange(ENTRIES, dtype=jnp.int32) // K_ACT
    entry_pick = (positions[:, None] == entry_pos[None, :]).astype(jnp.float32)
    target_rows = target_ids.reshape(LAYERS, TB)
    target_cols = target_pos.reshape(LAYERS, TB)
    row_count = LAYERS * TB * SEQ

    def layer_step(adjoint, layer_num):
        enc_rows = jnp.take(encoders[layer_num], target_rows[layer_num], axis=0).astype(jnp.float32)
        pos_hits = (positions[None, :] == target_cols[layer_num][:, None]).astype(jnp.float32)
        start_rows = pos_hits[:, :, None] * enc_rows[:, None, :]
        adjoint = lax.dynamic_update_index_in_dim(adjoint, start_rows, layer_num, 0)
        rounded = adjoint.astype(jnp.bfloat16).reshape(row_count, D)
        panels = jnp.take(decoders[layer_num], act_ids[layer_num], axis=0)
        edge_raw = jnp.dot(rounded, panels.T, preferred_element_type=jnp.float32).reshape(LAYERS * TB, SEQ, ENTRIES)
        edge_vals = jnp.sum(edge_raw * entry_pick[None], axis=1) * act_values[layer_num][None, :]
        head_grad = jnp.dot(rounded, out_proj[layer_num].T, preferred_element_type=jnp.float32)
        head_grad = head_grad.reshape(LAYERS * TB, SEQ, HEADS, HD)
        mixed_rows = jnp.einsum("hpq,bphk->hbqk", attention[layer_num], head_grad)
        mixed_rows = mixed_rows.astype(jnp.bfloat16).reshape(HEADS, row_count, HD)
        value_heads = value_proj[layer_num].reshape(D, HEADS, HD).transpose(1, 0, 2)
        scale_rows = jnp.tile(norm_scale[layer_num], LAYERS * TB)

        def head_step(summed, inputs):
            mixed_head, value_head = inputs
            head_term = jnp.dot(mixed_head, value_head.T, preferred_element_type=jnp.float32)
            head_term = (head_term * scale_rows[:, None]).astype(jnp.bfloat16)
            return summed + head_term.astype(jnp.float32), None

        summed, unused = lax.scan(head_step, jnp.zeros((row_count, D), jnp.float32), (mixed_rows, value_heads))
        adjoint = adjoint + summed.reshape(LAYERS, TB, SEQ, D)
        return adjoint, edge_vals

    layer_order = jnp.arange(LAYERS - 1, -1, -1, dtype=jnp.int32)
    final_state, edges_rev = lax.scan(layer_step, jnp.zeros((LAYERS, TB, SEQ, D), jnp.float32), layer_order)
    return edges_rev[::-1]
```

```python
import jax
import jax.numpy as jnp
from jax import lax
from jax.sharding import Mesh, PartitionSpec as P

K_ACT = 256
BF = jnp.bfloat16
F32 = jnp.float32
FEAT = ("y2", "par", "zh", "core")
CHIPS = ("y2", "par", "zh")
QUADS = 4
SWAP = [(0, 1), (1, 0)]


def neighbour_heads(shard):
    pairs = []
    for y in range(8):
        pairs.append((2 * y, 2 * ((y - 1) % 8)))
        pairs.append((2 * y + 1, 2 * ((y + 1) % 8) + 1))
    split = [(y * 2 + core) for y in range(8) for core in range(2)]
    assert len(split) == len(pairs)
    return lax.ppermute(shard, ("y2", "par", "core"), pairs)


def send_down(shard, step, by, sections):
    pairs = []
    for section in range(1, sections - step):
        for i in range(QUADS):
            pairs.append((section * QUADS + i, (section - 1) * QUADS + (i + by) % QUADS))
    return lax.ppermute(shard, ("section", "y2"), pairs)


def decoder_panel(dec_table, act_ids, entries_dev, feat_index, feat_count):
    feat_rows, model_width = dec_table.shape
    slot_count = 2 * entries_dev // feat_count
    ids_blocks = act_ids.reshape(feat_count, entries_dev)
    owner_ids = ids_blocks // feat_rows
    local_ids = ids_blocks % feat_rows
    owned_mask = owner_ids == feat_index
    entry_iota = jnp.arange(entries_dev, dtype=jnp.int32)
    before = (entry_iota[:, None] < entry_iota[None, :]).astype(BF)
    slot_rank = jnp.dot(owned_mask.astype(BF), before, preferred_element_type=F32).astype(jnp.int32)
    slot_iota = jnp.arange(slot_count, dtype=jnp.int32)
    selected = (
        owned_mask[:, None, :] & (slot_rank[:, None, :] == slot_iota[None, :, None])
    ).astype(jnp.int32)
    source_row = jnp.sum(selected * local_ids[:, None, :], axis=2)
    outgoing = jnp.take(dec_table, source_row.reshape(-1), axis=0).reshape(
        feat_count, slot_count, model_width
    )
    own_owner = lax.dynamic_index_in_dim(owner_ids, feat_index, 0, keepdims=False)
    earlier = (entry_iota[None, :] < entry_iota[:, None]).astype(jnp.int32)
    same_owner = (own_owner[:, None] == own_owner[None, :]).astype(jnp.int32)
    own_rank = jnp.sum(earlier * same_owner, axis=1)
    flat_index = own_owner * slot_count + own_rank
    incoming = lax.all_to_all(outgoing, FEAT, split_axis=0, concat_axis=0, tiled=True)
    return jnp.take(incoming.reshape(feat_count * slot_count, model_width), flat_index, axis=0)


def per_device(
    decoders,
    encoders,
    out_proj,
    value_proj,
    attention,
    norm_scale,
    act_ids,
    act_values,
    target_ids,
    target_pos,
):
    sections = lax.axis_size("section")
    section_index = lax.axis_index("section")
    feat_index = lax.axis_index(FEAT)
    feat_count = lax.axis_size(FEAT)
    model_width = decoders.shape[2]
    half = model_width // 2
    feat_rows = decoders.shape[1]
    seq_len = attention.shape[2]
    head_width = out_proj.shape[1]
    entries_dev = act_values.shape[1]
    targets = target_ids.shape[0]

    own = (out_proj[0], value_proj[0], attention[0, 0])
    beyond = tuple(lax.ppermute(a, "zh", SWAP) for a in own)
    near = tuple(neighbour_heads(a) for a in own)

    feat_iota = jnp.arange(feat_rows, dtype=jnp.int32)
    target_pick = (
        (target_ids - feat_index * feat_rows)[:, None] == feat_iota[None, :]
    ).astype(BF)
    enc_rows = jnp.dot(target_pick, encoders[0], preferred_element_type=F32).astype(BF)
    enc_send = jnp.broadcast_to(
        enc_rows.reshape(1, targets, 2, half), (QUADS, targets, 2, half)
    ).reshape(feat_count, half)
    enc_got = lax.all_to_all(enc_send, FEAT, split_axis=0, concat_axis=0, tiled=True)
    enc_row = jnp.sum(enc_got.astype(F32), axis=0)
    own_target = lax.axis_index(("par", "zh"))
    own_pos = lax.dynamic_index_in_dim(target_pos, own_target, 0, keepdims=False)
    positions = jnp.arange(seq_len, dtype=jnp.int32)
    rows = jnp.where((positions == own_pos)[:, None], enc_row[None, :], 0.0)

    far = tuple(neighbour_heads(a) for a in beyond)
    out_parts, value_parts, mix_parts = [], [], []
    for out_head, value_head, mix_head in (own, near, beyond, far):
        out_parts.append(
            lax.all_to_all(
                out_head.reshape(head_width, 2, half).transpose(1, 0, 2),
                "core",
                split_axis=0,
                concat_axis=0,
                tiled=True,
            ).reshape(2 * head_width, half)
        )
        got = lax.all_to_all(
            value_head.reshape(2, half, head_width), "core", split_axis=0, concat_axis=0, tiled=True
        )
        value_parts += [got[0], got[1]]
        mix_parts.append(lax.all_gather(mix_head, "core", axis=0))
    out_weight = jnp.concatenate(out_parts, axis=0)
    value_weight = jnp.concatenate(value_parts, axis=1)
    mixing = jnp.concatenate(mix_parts, axis=0)
    heads = mixing.shape[0]
    mix_wide = jnp.broadcast_to(
        mixing.transpose(1, 2, 0)[..., None], (seq_len, seq_len, heads, head_width)
    ).reshape(seq_len, seq_len, heads * head_width)
    scales = norm_scale[0][:, None]

    history = [rows.astype(BF)]
    for step in range(sections - 1):
        grad_part = lax.dot_general(
            history[-1], out_weight, (((1,), (1,)), ((), ())), preferred_element_type=F32
        )
        grads = jnp.sum(lax.all_gather(grad_part, "core", axis=0), axis=0)
        mixed = jnp.sum(mix_wide * grads[:, None, :], axis=0).astype(BF)
        term = lax.dot_general(
            mixed, value_weight, (((1,), (1,)), ((), ())), preferred_element_type=F32
        )
        share = (rows * (1.0 / QUADS) + term * scales).astype(BF)
        arrived = [send_down(share, step, by, sections) for by in range(QUADS)]
        rows = sum(a.astype(F32) for a in arrived)
        history.append(rows.astype(BF))

    panel = decoder_panel(decoders[0], act_ids[0], entries_dev, feat_index, feat_count)

    steps_each = sections // QUADS
    held = jnp.stack(history)
    first = lax.axis_index("y2") * steps_each
    held = lax.dynamic_slice_in_dim(held, first, steps_each, 0).transpose(1, 0, 2)
    got = lax.all_to_all(held, CHIPS, split_axis=0, concat_axis=0, tiled=True)
    got = lax.all_gather(got.reshape(-1, half), "core", axis=0)
    raw = sum(
        lax.dot_general(
            got[core],
            panel[:, core * half : (core + 1) * half],
            (((1,), (1,)), ((), ())),
            preferred_element_type=F32,
        )
        for core in range(2)
    )
    edges = raw.reshape(QUADS, targets, steps_each, entries_dev).transpose(0, 2, 1, 3)
    edges = edges.reshape(sections * targets, entries_dev) * act_values[0][None, :]
    padded = jnp.concatenate([jnp.zeros_like(edges), edges], axis=0)
    edges = lax.dynamic_slice_in_dim(
        padded, (sections - section_index) * targets, sections * targets, 0
    )
    return edges[None]


def solution(mesh):
    sections = mesh.shape["section"]
    fine = Mesh(mesh.devices.reshape(sections, 4, 2, 2, 2), ("section", *FEAT))
    in_specs = (
        P("section", FEAT, None),
        P("section", FEAT, None),
        P("section", FEAT, None),
        P("section", None, FEAT),
        P("section", FEAT, None, None),
        P("section", None),
        P("section", None),
        P("section", FEAT),
        P("section"),
        P("section"),
    )
    return jax.shard_map(
        per_device, mesh=fine, in_specs=in_specs, out_specs=P("section", None, FEAT), check_vma=False
    )
```

```python
import jax
import jax.numpy as jnp
from jax import lax
from jax.experimental import pallas as pl
from jax.experimental.pallas import tpu as pltpu
from jax.sharding import Mesh, PartitionSpec as P

K_ACT = 256
BF = jnp.bfloat16
F32 = jnp.float32
FEAT = ("y2", "par", "zh", "core")
CHIPS = ("y2", "par", "zh")
QUADS = 4
SWAP = [(0, 1), (1, 0)]


def neighbour_heads(shard):
    pairs = []
    for y in range(8):
        pairs.append((2 * y, 2 * ((y - 1) % 8)))
        pairs.append((2 * y + 1, 2 * ((y + 1) % 8) + 1))
    split = [(y * 2 + core) for y in range(8) for core in range(2)]
    assert len(split) == len(pairs)
    return lax.ppermute(shard, ("y2", "par", "core"), pairs)


def send_down(shard, by, sections):
    pairs = []
    for section in range(1, sections):
        for i in range(QUADS):
            pairs.append((section * QUADS + i, (section - 1) * QUADS + (i + by) % QUADS))
    return lax.ppermute(shard, ("section", "y2"), pairs)


def grads_kernel(*refs):
    *in_refs, rows_ref, rounded_ref, grads_ref = refs
    arrived, outs = in_refs[:QUADS], in_refs[QUADS:]
    rows = arrived[0][...].astype(F32)
    for ref in arrived[1:]:
        rows = rows + ref[...].astype(F32)
    rows_ref[...] = rows
    rounded = rows.astype(BF)
    rounded_ref[...] = rounded
    wide = outs[0].shape[0]
    for k, ref in enumerate(outs):
        grads_ref[:, k * wide : (k + 1) * wide] = lax.dot_general(
            rounded, ref[...], (((1,), (1,)), ((), ())), preferred_element_type=F32
        )


def terms_kernel(grads_ref, mix_ref, rows_ref, scales_ref, *refs):
    *values, share_ref = refs
    grads = grads_ref[0] + grads_ref[1]
    mixed = mix_ref[0] * grads[0:1, :]
    for p in range(1, grads.shape[0]):
        mixed = mixed + mix_ref[p] * grads[p : p + 1, :]
    mixed = mixed.astype(BF)
    wide = values[0].shape[1]
    term = None
    for k, ref in enumerate(values):
        part = lax.dot_general(
            mixed[:, k * wide : (k + 1) * wide],
            ref[...],
            (((1,), (1,)), ((), ())),
            preferred_element_type=F32,
        )
        term = part if term is None else term + part
    share_ref[...] = (rows_ref[...] * (1.0 / QUADS) + term * scales_ref[...]).astype(BF)


def keep(array):
    return pltpu.with_memory_space_constraint(array, pltpu.VMEM)


def whole():
    return pl.BlockSpec(memory_space=pltpu.VMEM)


def head_grads(arrived, outs):
    seq_len, half = arrived[0].shape
    heads_wide = sum(w.shape[0] for w in outs)
    return pl.pallas_call(
        grads_kernel,
        out_shape=(
            jax.ShapeDtypeStruct((seq_len, half), F32),
            jax.ShapeDtypeStruct((seq_len, half), BF),
            jax.ShapeDtypeStruct((seq_len, heads_wide), F32),
        ),
        in_specs=[whole()] * (len(arrived) + len(outs)),
        out_specs=(whole(),) * 3,
        compiler_params=pltpu.CompilerParams(vmem_limit_bytes=24 << 20),
        name="head_grads",
    )(*arrived, *outs)


def head_terms(grads, mix_wide, values, rows, scales):
    return pl.pallas_call(
        terms_kernel,
        out_shape=jax.ShapeDtypeStruct(rows.shape, BF),
        in_specs=[whole()] * (4 + len(values)),
        out_specs=whole(),
        compiler_params=pltpu.CompilerParams(vmem_limit_bytes=24 << 20),
        name="head_terms",
    )(grads, mix_wide, rows, scales, *values)


def decoder_panel(dec_table, act_ids, entries_dev, feat_index, feat_count):
    feat_rows, model_width = dec_table.shape
    slot_count = 2 * entries_dev // feat_count
    ids_blocks = act_ids.reshape(feat_count, entries_dev)
    owner_ids = ids_blocks // feat_rows
    local_ids = ids_blocks % feat_rows
    owned_mask = owner_ids == feat_index
    entry_iota = jnp.arange(entries_dev, dtype=jnp.int32)
    before = (entry_iota[:, None] < entry_iota[None, :]).astype(BF)
    slot_rank = jnp.dot(owned_mask.astype(BF), before, preferred_element_type=F32).astype(jnp.int32)
    slot_iota = jnp.arange(slot_count, dtype=jnp.int32)
    selected = (
        owned_mask[:, None, :] & (slot_rank[:, None, :] == slot_iota[None, :, None])
    ).astype(jnp.int32)
    source_row = jnp.sum(selected * local_ids[:, None, :], axis=2)
    outgoing = jnp.take(dec_table, source_row.reshape(-1), axis=0).reshape(
        feat_count, slot_count, model_width
    )
    own_owner = lax.dynamic_index_in_dim(owner_ids, feat_index, 0, keepdims=False)
    earlier = (entry_iota[None, :] < entry_iota[:, None]).astype(jnp.int32)
    same_owner = (own_owner[:, None] == own_owner[None, :]).astype(jnp.int32)
    own_rank = jnp.sum(earlier * same_owner, axis=1)
    flat_index = own_owner * slot_count + own_rank
    incoming = lax.all_to_all(outgoing, FEAT, split_axis=0, concat_axis=0, tiled=True)
    return jnp.take(incoming.reshape(feat_count * slot_count, model_width), flat_index, axis=0)


def per_device(
    decoders,
    encoders,
    out_proj,
    value_proj,
    attention,
    norm_scale,
    act_ids,
    act_values,
    target_ids,
    target_pos,
):
    sections = lax.axis_size("section")
    section_index = lax.axis_index("section")
    feat_index = lax.axis_index(FEAT)
    feat_count = lax.axis_size(FEAT)
    model_width = decoders.shape[2]
    half = model_width // 2
    feat_rows = decoders.shape[1]
    seq_len = attention.shape[2]
    head_width = out_proj.shape[1]
    entries_dev = act_values.shape[1]
    targets = target_ids.shape[0]

    own = (out_proj[0], value_proj[0], attention[0, 0])
    beyond = tuple(lax.ppermute(a, "zh", SWAP) for a in own)
    near = tuple(neighbour_heads(a) for a in own)

    feat_iota = jnp.arange(feat_rows, dtype=jnp.int32)
    target_pick = (
        (target_ids - feat_index * feat_rows)[:, None] == feat_iota[None, :]
    ).astype(BF)
    enc_rows = jnp.dot(target_pick, encoders[0], preferred_element_type=F32).astype(BF)
    enc_send = jnp.broadcast_to(
        enc_rows.reshape(1, targets, 2, half), (QUADS, targets, 2, half)
    ).reshape(feat_count, half)
    enc_got = lax.all_to_all(enc_send, FEAT, split_axis=0, concat_axis=0, tiled=True)
    enc_row = jnp.sum(enc_got.astype(F32), axis=0)
    own_target = lax.axis_index(("par", "zh"))
    own_pos = lax.dynamic_index_in_dim(target_pos, own_target, 0, keepdims=False)
    positions = jnp.arange(seq_len, dtype=jnp.int32)
    rows = jnp.where((positions == own_pos)[:, None], enc_row[None, :], 0.0)

    panel = decoder_panel(decoders[0], act_ids[0], entries_dev, feat_index, feat_count)
    rows, panel = lax.optimization_barrier((rows, panel))
    far = tuple(neighbour_heads(a) for a in beyond)
    outs, values, mix_parts = [], [], []
    for out_head, value_head, mix_head in (own, near, beyond, far):
        halves = jnp.stack([out_head[:, :half], out_head[:, half:]])
        outs.append(
            lax.all_to_all(halves, "core", split_axis=0, concat_axis=0, tiled=True).reshape(
                2 * head_width, half
            )
        )
        got = lax.all_to_all(
            value_head.reshape(2, half, head_width), "core", split_axis=0, concat_axis=0, tiled=True
        )
        values.append(jnp.concatenate([got[0], got[1]], axis=1))
        mix_parts.append(lax.all_gather(mix_head, "core", axis=0))
    mixing = jnp.concatenate(mix_parts, axis=0)
    heads = mixing.shape[0]
    mix_wide = jnp.broadcast_to(
        mixing.transpose(1, 2, 0)[..., None], (seq_len, seq_len, heads, head_width)
    ).reshape(seq_len, seq_len, heads * head_width)
    scales = norm_scale[0][:, None]

    outs, values = [keep(w) for w in outs], [keep(w) for w in values]
    mix_wide = keep(mix_wide)
    arrived = [rows.astype(BF)] + [jnp.zeros((seq_len, half), BF)] * (QUADS - 1)
    history = [arrived[0]]
    for step in range(sections - 1):
        rows, rounded, grad_part = head_grads(arrived, outs)
        if step:
            history.append(rounded)
        grads = lax.all_gather(grad_part, "core", axis=0)
        share = head_terms(grads, mix_wide, values, rows, scales)
        arrived = [send_down(share, by, sections) for by in range(QUADS)]
    history.append(sum(a.astype(F32) for a in arrived).astype(BF))

    steps_each = sections // QUADS
    held = jnp.stack(history)
    first = lax.axis_index("y2") * steps_each
    held = lax.dynamic_slice_in_dim(held, first, steps_each, 0).transpose(1, 0, 2)
    got = lax.all_to_all(held, CHIPS, split_axis=0, concat_axis=0, tiled=True)
    got = lax.all_gather(got.reshape(-1, half), "core", axis=0)
    raw = sum(
        lax.dot_general(
            got[core],
            panel[:, core * half : (core + 1) * half],
            (((1,), (1,)), ((), ())),
            preferred_element_type=F32,
        )
        for core in range(2)
    )
    edges = raw.reshape(QUADS, targets, steps_each, entries_dev).transpose(0, 2, 1, 3)
    edges = edges.reshape(sections * targets, entries_dev) * act_values[0][None, :]
    padded = jnp.concatenate([jnp.zeros_like(edges), edges], axis=0)
    edges = lax.dynamic_slice_in_dim(
        padded, (sections - section_index) * targets, sections * targets, 0
    )
    return edges[None]


def solution(mesh):
    sections = mesh.shape["section"]
    fine = Mesh(mesh.devices.reshape(sections, 4, 2, 2, 2), ("section", *FEAT))
    in_specs = (
        P("section", FEAT, None),
        P("section", FEAT, None),
        P("section", FEAT, None),
        P("section", None, FEAT),
        P("section", FEAT, None, None),
        P("section", None),
        P("section", None),
        P("section", FEAT),
        P("section"),
        P("section"),
    )
    return jax.shard_map(
        per_device, mesh=fine, in_specs=in_specs, out_specs=P("section", None, FEAT), check_vma=False
    )
```

```python
import jax
import jax.numpy as jnp
from jax import lax
from jax.experimental import pallas as pl
from jax.experimental.pallas import tpu as pltpu
from jax.sharding import Mesh, PartitionSpec as P

K_ACT = 256
BF = jnp.bfloat16
F32 = jnp.float32
FEAT = ("y2", "par", "zh", "core")
CHIPS = ("y2", "par", "zh")
QUADS = 4
PANEL_BY = 5
SWAP = [(0, 1), (1, 0)]


def neighbour_heads(shard):
    pairs = []
    for y in range(8):
        pairs.append((2 * y, 2 * ((y - 1) % 8)))
        pairs.append((2 * y + 1, 2 * ((y + 1) % 8) + 1))
    split = [(y * 2 + core) for y in range(8) for core in range(2)]
    assert len(split) == len(pairs)
    return lax.ppermute(shard, ("y2", "par", "core"), pairs)


def send_down(shard, turn, sections):
    places = {0: ((0, 0), (3, 1)), 1: ((2, 1), (1, 0))}[turn]
    pairs = []
    for section in range(1, sections):
        for i in range(QUADS):
            for core, (by, to_core) in enumerate(places):
                below = (section - 1) * QUADS + (i + by) % QUADS
                pairs.append(((section * QUADS + i) * 2 + core, below * 2 + to_core))
    return lax.ppermute(shard, ("section", "y2", "core"), pairs)


def grads_kernel(first_ref, second_ref, *refs):
    *outs, part_ref, rounded_ref, grads_ref = refs
    part = first_ref[...].astype(F32) + second_ref[...].astype(F32)
    part_ref[...] = part
    rounded = part.astype(BF)
    rounded_ref[...] = rounded
    wide = outs[0].shape[0]
    for k, ref in enumerate(outs):
        grads_ref[:, k * wide : (k + 1) * wide] = lax.dot_general(
            rounded, ref[...], (((1,), (1,)), ((), ())), preferred_element_type=F32
        )


def terms_kernel(core_ref, grads_ref, mix_ref, part_ref, scales_ref, *refs):
    *values, share_ref = refs
    core = core_ref[0]
    mine, other = grads_ref[core], grads_ref[1 - core]
    wide = values[0].shape[1]
    head = wide // 2
    swapped = []
    for k in range(len(values)):
        swapped.append(other[:, k * wide + head : (k + 1) * wide])
        swapped.append(other[:, k * wide : k * wide + head])
    grads = mine + jnp.concatenate(swapped, axis=1)
    mixed = mix_ref[0] * grads[0:1, :]
    for p in range(1, grads.shape[0]):
        mixed = mixed + mix_ref[p] * grads[p : p + 1, :]
    mixed = mixed.astype(BF)
    term = None
    for k, ref in enumerate(values):
        product = lax.dot_general(
            mixed[:, k * wide : (k + 1) * wide],
            ref[...],
            (((1,), (1,)), ((), ())),
            preferred_element_type=F32,
        )
        term = product if term is None else term + product
    share_ref[...] = (part_ref[...] * 0.5 + term * scales_ref[...]).astype(BF)


def keep(array):
    return pltpu.with_memory_space_constraint(array, pltpu.VMEM)


def whole():
    return pl.BlockSpec(memory_space=pltpu.VMEM)


def head_grads(arrived, outs):
    seq_len, model_width = arrived[0].shape
    heads_wide = sum(w.shape[0] for w in outs)
    return pl.pallas_call(
        grads_kernel,
        out_shape=(
            jax.ShapeDtypeStruct((seq_len, model_width), F32),
            jax.ShapeDtypeStruct((seq_len, model_width), BF),
            jax.ShapeDtypeStruct((seq_len, heads_wide), F32),
        ),
        in_specs=[whole()] * (2 + len(outs)),
        out_specs=(whole(),) * 3,
        compiler_params=pltpu.CompilerParams(vmem_limit_bytes=24 << 20),
        name="head_grads",
    )(*arrived, *outs)


def head_terms(core, grads, mix_wide, part, scales, values):
    return pl.pallas_call(
        terms_kernel,
        out_shape=jax.ShapeDtypeStruct(part.shape, BF),
        in_specs=[pl.BlockSpec(memory_space=pltpu.SMEM)] + [whole()] * (4 + len(values)),
        out_specs=whole(),
        compiler_params=pltpu.CompilerParams(vmem_limit_bytes=24 << 20),
        name="head_terms",
    )(core, grads, mix_wide, part, scales, *values)


def panel_route(dec_table, act_ids, entries_dev, feat_index, feat_count):
    feat_rows, model_width = dec_table.shape
    slot_count = 2 * entries_dev // feat_count
    ids_blocks = act_ids.reshape(feat_count, entries_dev)
    owner_ids = ids_blocks // feat_rows
    local_ids = ids_blocks % feat_rows
    owned_mask = owner_ids == feat_index
    entry_iota = jnp.arange(entries_dev, dtype=jnp.int32)
    before = (entry_iota[:, None] < entry_iota[None, :]).astype(BF)
    slot_rank = jnp.dot(owned_mask.astype(BF), before, preferred_element_type=F32).astype(jnp.int32)
    slot_iota = jnp.arange(slot_count, dtype=jnp.int32)
    selected = (
        owned_mask[:, None, :] & (slot_rank[:, None, :] == slot_iota[None, :, None])
    ).astype(jnp.int32)
    source_row = jnp.sum(selected * local_ids[:, None, :], axis=2)
    outgoing = jnp.take(dec_table, source_row.reshape(-1), axis=0).reshape(
        feat_count, slot_count, model_width
    )
    own_owner = lax.dynamic_index_in_dim(owner_ids, feat_index, 0, keepdims=False)
    earlier = (entry_iota[None, :] < entry_iota[:, None]).astype(jnp.int32)
    same_owner = (own_owner[:, None] == own_owner[None, :]).astype(jnp.int32)
    own_rank = jnp.sum(earlier * same_owner, axis=1)
    flat_index = own_owner * slot_count + own_rank
    return outgoing, flat_index


def per_device(
    decoders,
    encoders,
    out_proj,
    value_proj,
    attention,
    norm_scale,
    act_ids,
    act_values,
    target_ids,
    target_pos,
):
    sections = lax.axis_size("section")
    section_index = lax.axis_index("section")
    feat_index = lax.axis_index(FEAT)
    feat_count = lax.axis_size(FEAT)
    model_width = decoders.shape[2]
    half = model_width // 2
    feat_rows = decoders.shape[1]
    seq_len = attention.shape[2]
    head_width = out_proj.shape[1]
    entries_dev = act_values.shape[1]
    targets = target_ids.shape[0]

    own = (out_proj[0], value_proj[0])
    own_mix = attention[0, 0]
    beyond = tuple(lax.ppermute(a, "zh", SWAP) for a in own)
    near = tuple(neighbour_heads(a) for a in own)

    feat_iota = jnp.arange(feat_rows, dtype=jnp.int32)
    target_pick = (
        (target_ids - feat_index * feat_rows)[:, None] == feat_iota[None, :]
    ).astype(BF)
    enc_rows = jnp.dot(target_pick, encoders[0], preferred_element_type=F32).astype(BF)
    enc_send = jnp.broadcast_to(
        enc_rows[None, :, None, :], (QUADS, targets, 2, model_width)
    ).reshape(feat_count, model_width)
    near, own, own_mix, enc_send = lax.optimization_barrier((near, own, own_mix, enc_send))
    beyond_mix = lax.ppermute(own_mix, "zh", SWAP)
    near_mix = neighbour_heads(own_mix)
    far_mix = neighbour_heads(beyond_mix)
    enc_got = lax.all_to_all(enc_send, FEAT, split_axis=0, concat_axis=0, tiled=True)
    enc_row = jnp.sum(enc_got.astype(F32), axis=0)
    own_target = lax.axis_index(("par", "zh"))
    own_pos = lax.dynamic_index_in_dim(target_pos, own_target, 0, keepdims=False)
    positions = jnp.arange(seq_len, dtype=jnp.int32)
    start = jnp.where((positions == own_pos)[:, None], enc_row[None, :], 0.0)

    outgoing, flat_index = panel_route(
        decoders[0], act_ids[0], entries_dev, feat_index, feat_count
    )
    far = tuple(neighbour_heads(a) for a in beyond)
    far, outgoing = lax.optimization_barrier((far, outgoing))
    incoming = lax.all_to_all(outgoing, FEAT, split_axis=0, concat_axis=0, tiled=True)

    outs, values = [], []
    for out_head, value_head in (own, near, beyond, far):
        outs.append(jnp.concatenate([out_head, lax.ppermute(out_head, "core", SWAP)], axis=0))
        values.append(
            jnp.concatenate([value_head, lax.ppermute(value_head, "core", SWAP)], axis=1)
        )
    core_mix = jnp.stack([own_mix, near_mix, beyond_mix, far_mix])
    mixing = jnp.stack([core_mix, lax.ppermute(core_mix, "core", SWAP)], axis=1)
    mixing = mixing.reshape(-1, seq_len, seq_len)
    heads = mixing.shape[0]
    mix_wide = jnp.broadcast_to(
        mixing.transpose(1, 2, 0)[..., None], (seq_len, seq_len, heads, head_width)
    ).reshape(seq_len, seq_len, heads * head_width)
    scales = norm_scale[0][:, None]

    outs, values = [keep(w) for w in outs], [keep(w) for w in values]
    mix_wide = keep(mix_wide)
    core = lax.axis_index("core").reshape(1)
    quarter = (start * 0.25).astype(BF)
    arrived = (quarter, quarter)
    history = []
    for step in range(sections - 1):
        if step == PANEL_BY:
            arrived, incoming = lax.optimization_barrier((arrived, incoming))
        part, rounded, grad_part = head_grads(arrived, outs)
        history.append(rounded)
        grads = lax.all_gather(grad_part, "core", axis=0)
        share = head_terms(core, grads, mix_wide, part, scales, values)
        arrived = tuple(send_down(share, turn, sections) for turn in range(2))
    history.append((arrived[0].astype(F32) + arrived[1].astype(F32)).astype(BF))
    panel = jnp.take(incoming.reshape(-1, model_width), flat_index, axis=0)

    steps_each = sections // QUADS
    held = jnp.stack(history)
    first = lax.axis_index("y2") * steps_each
    held = lax.dynamic_slice_in_dim(held, first, steps_each, 0).transpose(1, 0, 2)
    this_half = lax.dynamic_slice_in_dim(held, core[0] * half, half, 2)
    other_half = lax.dynamic_slice_in_dim(held, (1 - core[0]) * half, half, 2)
    got_half = lax.ppermute(other_half, "core", SWAP)
    held = (this_half.astype(F32) + got_half.astype(F32)).astype(BF)
    got = lax.all_to_all(held, CHIPS, split_axis=0, concat_axis=0, tiled=True)
    got = lax.all_gather(got.reshape(-1, half), "core", axis=0)
    raw = sum(
        lax.dot_general(
            got[side],
            panel[:, side * half : (side + 1) * half],
            (((1,), (1,)), ((), ())),
            preferred_element_type=F32,
        )
        for side in range(2)
    )
    edges = raw.reshape(QUADS, targets, steps_each, entries_dev).transpose(0, 2, 1, 3)
    edges = edges.reshape(sections * targets, entries_dev) * act_values[0][None, :]
    padded = jnp.concatenate([jnp.zeros_like(edges), edges], axis=0)
    edges = lax.dynamic_slice_in_dim(
        padded, (sections - section_index) * targets, sections * targets, 0
    )
    return edges[None]


def solution(mesh):
    sections = mesh.shape["section"]
    fine = Mesh(mesh.devices.reshape(sections, 4, 2, 2, 2), ("section", *FEAT))
    in_specs = (
        P("section", FEAT, None),
        P("section", FEAT, None),
        P("section", FEAT, None),
        P("section", None, FEAT),
        P("section", FEAT, None, None),
        P("section", None),
        P("section", None),
        P("section", FEAT),
        P("section"),
        P("section"),
    )
    return jax.shard_map(
        per_device, mesh=fine, in_specs=in_specs, out_specs=P("section", None, FEAT), check_vma=False
    )
```

```python
import jax
import jax.numpy as jnp
from jax import lax
from jax.experimental import pallas as pl
from jax.experimental.pallas import tpu as pltpu
from jax.sharding import Mesh, PartitionSpec as P

K_ACT = 256
BF = jnp.bfloat16
F32 = jnp.float32
FEAT = ("y2", "par", "zh", "core")
CHIPS = ("y2", "par", "zh")
QUADS = 4
PANEL_BY = 5
SWAP = [(0, 1), (1, 0)]


def neighbour_heads(shard):
    pairs = []
    for y in range(8):
        pairs.append((2 * y, 2 * ((y - 1) % 8)))
        pairs.append((2 * y + 1, 2 * ((y + 1) % 8) + 1))
    split = [(y * 2 + core) for y in range(8) for core in range(2)]
    assert len(split) == len(pairs)
    return lax.ppermute(shard, ("y2", "par", "core"), pairs)


def send_down(shard, turn, sections):
    places = {0: ((0, 0), (3, 1)), 1: ((2, 1), (1, 0))}[turn]
    pairs = []
    for section in range(1, sections):
        for i in range(QUADS):
            for core, (by, to_core) in enumerate(places):
                below = (section - 1) * QUADS + (i + by) % QUADS
                pairs.append(((section * QUADS + i) * 2 + core, below * 2 + to_core))
    return lax.ppermute(shard, ("section", "y2", "core"), pairs)


def grads_kernel(first_ref, second_ref, *refs):
    *outs, part_ref, rounded_ref, grads_ref = refs
    part = first_ref[...].astype(F32) + second_ref[...].astype(F32)
    part_ref[...] = part
    rounded = part.astype(BF)
    rounded_ref[...] = rounded
    wide = outs[0].shape[1]
    for k, ref in enumerate(outs):
        grads_ref[:, k * wide : (k + 1) * wide] = jnp.dot(
            rounded, ref[...], preferred_element_type=F32
        )


def terms_kernel(core_ref, grads_ref, mix_ref, part_ref, scales_ref, *refs):
    *values, share_ref = refs
    core = core_ref[0]
    mine, other = grads_ref[core], grads_ref[1 - core]
    head = values[0].shape[0] // 2
    swapped = []
    for k in range(len(values)):
        swapped.append(other[:, (k ^ 1) * head : ((k ^ 1) + 1) * head])
    grads = mine + jnp.concatenate(swapped, axis=1)
    mixed = mix_ref[0] * grads[0:1, :]
    for p in range(1, grads.shape[0]):
        mixed = mixed + mix_ref[p] * grads[p : p + 1, :]
    mixed = mixed.astype(BF)
    term = None
    for k, ref in enumerate(values):
        product = jnp.dot(
            mixed[:, k * head : (k + 1) * head],
            ref[head : 2 * head, :],
            preferred_element_type=F32,
        )
        term = product if term is None else term + product
    share_ref[...] = (part_ref[...] * 0.5 + term * scales_ref[...]).astype(BF)


def turn_kernel(mine_ref, other_ref, turned_ref):
    head = mine_ref.shape[0] // 2
    turned_ref[:, :head] = mine_ref[:head, :].T
    turned_ref[:, head:] = other_ref[:head, :].T


def keep(array):
    return pltpu.with_memory_space_constraint(array, pltpu.VMEM)


def whole():
    return pl.BlockSpec(memory_space=pltpu.VMEM)


def prepare(mine):
    other = lax.ppermute(mine, "core", SWAP)
    turned = pl.pallas_call(
        turn_kernel,
        out_shape=jax.ShapeDtypeStruct((mine.shape[1], mine.shape[0]), BF),
        in_specs=[whole()] * 2,
        out_specs=whole(),
        compiler_params=pltpu.CompilerParams(vmem_limit_bytes=24 << 20),
        name="turn_heads",
    )(keep(mine), keep(other))
    return turned, mine, other


def head_grads(arrived, outs):
    seq_len, model_width = arrived[0].shape
    heads_wide = sum(w.shape[1] for w in outs)
    return pl.pallas_call(
        grads_kernel,
        out_shape=(
            jax.ShapeDtypeStruct((seq_len, model_width), F32),
            jax.ShapeDtypeStruct((seq_len, model_width), BF),
            jax.ShapeDtypeStruct((seq_len, heads_wide), F32),
        ),
        in_specs=[whole()] * (2 + len(outs)),
        out_specs=(whole(),) * 3,
        compiler_params=pltpu.CompilerParams(vmem_limit_bytes=24 << 20),
        name="head_grads",
    )(*arrived, *outs)


def head_terms(core, grads, mix_wide, part, scales, values):
    return pl.pallas_call(
        terms_kernel,
        out_shape=jax.ShapeDtypeStruct(part.shape, BF),
        in_specs=[pl.BlockSpec(memory_space=pltpu.SMEM)] + [whole()] * (4 + len(values)),
        out_specs=whole(),
        compiler_params=pltpu.CompilerParams(vmem_limit_bytes=24 << 20),
        name="head_terms",
    )(core, grads, mix_wide, part, scales, *values)


def panel_route(dec_table, act_ids, entries_dev, feat_index, feat_count):
    feat_rows, model_width = dec_table.shape
    slot_count = 2 * entries_dev // feat_count
    ids_blocks = act_ids.reshape(feat_count, entries_dev)
    owner_ids = ids_blocks // feat_rows
    local_ids = ids_blocks % feat_rows
    owned_mask = owner_ids == feat_index
    entry_iota = jnp.arange(entries_dev, dtype=jnp.int32)
    before = (entry_iota[:, None] < entry_iota[None, :]).astype(BF)
    slot_rank = jnp.dot(owned_mask.astype(BF), before, preferred_element_type=F32).astype(jnp.int32)
    slot_iota = jnp.arange(slot_count, dtype=jnp.int32)
    selected = (
        owned_mask[:, None, :] & (slot_rank[:, None, :] == slot_iota[None, :, None])
    ).astype(jnp.int32)
    source_row = jnp.sum(selected * local_ids[:, None, :], axis=2)
    outgoing = jnp.take(dec_table, source_row.reshape(-1), axis=0).reshape(
        feat_count, slot_count, model_width
    )
    own_owner = lax.dynamic_index_in_dim(owner_ids, feat_index, 0, keepdims=False)
    earlier = (entry_iota[None, :] < entry_iota[:, None]).astype(jnp.int32)
    same_owner = (own_owner[:, None] == own_owner[None, :]).astype(jnp.int32)
    own_rank = jnp.sum(earlier * same_owner, axis=1)
    flat_index = own_owner * slot_count + own_rank
    return outgoing, flat_index


def per_device(
    decoders,
    encoders,
    out_proj,
    value_proj,
    attention,
    norm_scale,
    act_ids,
    act_values,
    target_ids,
    target_pos,
):
    sections = lax.axis_size("section")
    section_index = lax.axis_index("section")
    feat_index = lax.axis_index(FEAT)
    feat_count = lax.axis_size(FEAT)
    model_width = decoders.shape[2]
    half = model_width // 2
    feat_rows = decoders.shape[1]
    seq_len = attention.shape[2]
    head_width = out_proj.shape[1]
    entries_dev = act_values.shape[1]
    targets = target_ids.shape[0]

    own = jnp.concatenate([out_proj[0], value_proj[0].T], axis=0)
    own_mix = attention[0, 0]
    beyond = lax.ppermute(own, "zh", SWAP)
    near = neighbour_heads(own)

    feat_iota = jnp.arange(feat_rows, dtype=jnp.int32)
    target_pick = (
        (target_ids - feat_index * feat_rows)[:, None] == feat_iota[None, :]
    ).astype(BF)
    enc_rows = jnp.dot(target_pick, encoders[0], preferred_element_type=F32).astype(BF)
    enc_send = jnp.broadcast_to(
        enc_rows[None, :, None, :], (QUADS, targets, 2, model_width)
    ).reshape(feat_count, model_width)
    beyond_mix = lax.ppermute(own_mix, "zh", SWAP)
    near_mix = neighbour_heads(own_mix)
    enc_got = lax.all_to_all(enc_send, FEAT, split_axis=0, concat_axis=0, tiled=True)
    outgoing, flat_index = panel_route(
        decoders[0], act_ids[0], entries_dev, feat_index, feat_count
    )
    own, beyond, near, beyond_mix, near_mix, enc_got, outgoing = lax.optimization_barrier(
        (own, beyond, near, beyond_mix, near_mix, enc_got, outgoing)
    )
    far = neighbour_heads(beyond)
    far_mix = neighbour_heads(beyond_mix)
    enc_row = jnp.sum(enc_got.astype(F32), axis=0)
    own_target = lax.axis_index(("par", "zh"))
    own_pos = lax.dynamic_index_in_dim(target_pos, own_target, 0, keepdims=False)
    positions = jnp.arange(seq_len, dtype=jnp.int32)
    start = jnp.where((positions == own_pos)[:, None], enc_row[None, :], 0.0)

    groups = [prepare(head) for head in (own, near, beyond)]
    core_mix = jnp.stack([own_mix, near_mix, beyond_mix, far_mix])
    mixing = jnp.stack([core_mix, lax.ppermute(core_mix, "core", SWAP)], axis=1)
    mixing = mixing.reshape(-1, seq_len, seq_len)
    heads = mixing.shape[0]
    mix_wide = jnp.broadcast_to(
        mixing.transpose(1, 2, 0)[..., None], (seq_len, seq_len, heads, head_width)
    ).reshape(seq_len, seq_len, heads * head_width)
    quarter = (start * 0.25).astype(BF)
    far, groups, mix_wide, quarter, outgoing = lax.optimization_barrier(
        (far, groups, mix_wide, quarter, outgoing)
    )
    incoming = lax.all_to_all(outgoing, FEAT, split_axis=0, concat_axis=0, tiled=True)
    panel = jnp.take(incoming.reshape(-1, model_width), flat_index, axis=0)
    groups.append(prepare(far))
    outs = [group[0] for group in groups]
    values = [head for group in groups for head in group[1:]]
    scales = norm_scale[0][:, None]

    outs, values = [keep(w) for w in outs], [keep(w) for w in values]
    mix_wide = keep(mix_wide)
    core = lax.axis_index("core").reshape(1)
    arrived = (quarter, quarter)
    history = []
    for step in range(sections - 1):
        if step == PANEL_BY:
            arrived, panel = lax.optimization_barrier((arrived, panel))
        part, rounded, grad_part = head_grads(arrived, outs)
        history.append(rounded)
        grads = lax.all_gather(grad_part, "core", axis=0)
        share = head_terms(core, grads, mix_wide, part, scales, values)
        arrived = tuple(send_down(share, turn, sections) for turn in (1, 0))
    history.append((arrived[0].astype(F32) + arrived[1].astype(F32)).astype(BF))

    steps_each = sections // QUADS
    held = jnp.stack(history)
    first = lax.axis_index("y2") * steps_each
    held = lax.dynamic_slice_in_dim(held, first, steps_each, 0).transpose(1, 0, 2)
    this_half = lax.dynamic_slice_in_dim(held, core[0] * half, half, 2)
    other_half = lax.dynamic_slice_in_dim(held, (1 - core[0]) * half, half, 2)
    got_half = lax.ppermute(other_half, "core", SWAP)
    held = (this_half.astype(F32) + got_half.astype(F32)).astype(BF)
    got = lax.all_to_all(held, CHIPS, split_axis=0, concat_axis=0, tiled=True)
    got = lax.all_gather(got.reshape(-1, half), "core", axis=0)
    raw = sum(
        lax.dot_general(
            got[side],
            panel[:, side * half : (side + 1) * half],
            (((1,), (1,)), ((), ())),
            preferred_element_type=F32,
        )
        for side in range(2)
    )
    edges = raw.reshape(QUADS, targets, steps_each, entries_dev).transpose(0, 2, 1, 3)
    edges = edges.reshape(sections * targets, entries_dev) * act_values[0][None, :]
    padded = jnp.concatenate([jnp.zeros_like(edges), edges], axis=0)
    edges = lax.dynamic_slice_in_dim(
        padded, (sections - section_index) * targets, sections * targets, 0
    )
    return edges[None]


def solution(mesh):
    sections = mesh.shape["section"]
    fine = Mesh(mesh.devices.reshape(sections, 4, 2, 2, 2), ("section", *FEAT))
    in_specs = (
        P("section", FEAT, None),
        P("section", FEAT, None),
        P("section", FEAT, None),
        P("section", None, FEAT),
        P("section", FEAT, None, None),
        P("section", None),
        P("section", None),
        P("section", FEAT),
        P("section"),
        P("section"),
    )
    return jax.shard_map(
        per_device, mesh=fine, in_specs=in_specs, out_specs=P("section", None, FEAT), check_vma=False
    )
```

```python
import jax
import jax.numpy as jnp
from jax import lax
from jax.experimental import pallas as pl
from jax.experimental.pallas import tpu as pltpu
from jax.sharding import Mesh, PartitionSpec as P

K_ACT = 256
BF = jnp.bfloat16
F32 = jnp.float32
FEAT = ("y2", "par", "zh", "core")
CHIPS = ("y2", "par", "zh")
QUADS = 4
PANEL_BY = 5
SWAP = [(0, 1), (1, 0)]


def neighbour_heads(shard):
    pairs = []
    for y in range(8):
        pairs.append((2 * y, 2 * ((y - 1) % 8)))
        pairs.append((2 * y + 1, 2 * ((y + 1) % 8) + 1))
    split = [(y * 2 + core) for y in range(8) for core in range(2)]
    assert len(split) == len(pairs)
    return lax.ppermute(shard, ("y2", "par", "core"), pairs)


def send_down(shard, turn, sections):
    places = {0: ((0, 0), (3, 1)), 1: ((2, 1), (1, 0))}[turn]
    pairs = []
    for section in range(1, sections):
        for i in range(QUADS):
            for core, (by, to_core) in enumerate(places):
                below = (section - 1) * QUADS + (i + by) % QUADS
                pairs.append(((section * QUADS + i) * 2 + core, below * 2 + to_core))
    return lax.ppermute(shard, ("section", "y2", "core"), pairs)


def grads_kernel(first_ref, second_ref, *refs):
    *outs, part_ref, rounded_ref, grads_ref = refs
    part = first_ref[...].astype(F32) + second_ref[...].astype(F32)
    part_ref[...] = part
    rounded = part.astype(BF)
    rounded_ref[...] = rounded
    wide = outs[0].shape[1]
    for k, ref in enumerate(outs):
        grads_ref[:, k * wide : (k + 1) * wide] = jnp.dot(
            rounded, ref[...], preferred_element_type=F32
        )


def terms_kernel(core_ref, grads_ref, mix_ref, part_ref, scales_ref, *refs):
    *values, share_ref = refs
    core = core_ref[0]
    mine, other = grads_ref[core], grads_ref[1 - core]
    wide = values[0].shape[0]
    head = wide // 2
    swapped = []
    for k in range(2 * len(values)):
        swapped.append(other[:, (k ^ 1) * head : ((k ^ 1) + 1) * head])
    grads = mine + jnp.concatenate(swapped, axis=1)
    mixed = mix_ref[0] * grads[0:1, :]
    for p in range(1, grads.shape[0]):
        mixed = mixed + mix_ref[p] * grads[p : p + 1, :]
    mixed = mixed.astype(BF)
    term = None
    for k, ref in enumerate(values):
        product = jnp.dot(
            mixed[:, k * wide : (k + 1) * wide],
            ref[...],
            preferred_element_type=F32,
        )
        term = product if term is None else term + product
    share_ref[...] = (part_ref[...] * 0.5 + term * scales_ref[...]).astype(BF)


def turn_kernel(mine_ref, other_ref, turned_ref, values_ref):
    head = mine_ref.shape[0] // 2
    turned_ref[:, :head] = mine_ref[:head, :].T
    turned_ref[:, head:] = other_ref[:head, :].T
    values_ref[:head, :] = mine_ref[head:, :]
    values_ref[head:, :] = other_ref[head:, :]


def keep(array):
    return pltpu.with_memory_space_constraint(array, pltpu.VMEM)


def whole():
    return pl.BlockSpec(memory_space=pltpu.VMEM)


def prepare(mine):
    other = lax.ppermute(mine, "core", SWAP)
    rows, model_width = mine.shape
    return pl.pallas_call(
        turn_kernel,
        out_shape=(
            jax.ShapeDtypeStruct((model_width, rows), BF),
            jax.ShapeDtypeStruct((rows, model_width), BF),
        ),
        in_specs=[whole()] * 2,
        out_specs=(whole(),) * 2,
        compiler_params=pltpu.CompilerParams(vmem_limit_bytes=24 << 20),
        name="turn_heads",
    )(mine, other)


def head_grads(arrived, outs):
    seq_len, model_width = arrived[0].shape
    heads_wide = sum(w.shape[1] for w in outs)
    return pl.pallas_call(
        grads_kernel,
        out_shape=(
            jax.ShapeDtypeStruct((seq_len, model_width), F32),
            jax.ShapeDtypeStruct((seq_len, model_width), BF),
            jax.ShapeDtypeStruct((seq_len, heads_wide), F32),
        ),
        in_specs=[whole()] * (2 + len(outs)),
        out_specs=(whole(),) * 3,
        compiler_params=pltpu.CompilerParams(vmem_limit_bytes=24 << 20),
        name="head_grads",
    )(*arrived, *outs)


def head_terms(core, grads, mix_wide, part, scales, values):
    return pl.pallas_call(
        terms_kernel,
        out_shape=jax.ShapeDtypeStruct(part.shape, BF),
        in_specs=[pl.BlockSpec(memory_space=pltpu.SMEM)] + [whole()] * (4 + len(values)),
        out_specs=whole(),
        compiler_params=pltpu.CompilerParams(vmem_limit_bytes=24 << 20),
        name="head_terms",
    )(core, grads, mix_wide, part, scales, *values)


def panel_route(dec_table, act_ids, entries_dev, feat_index, feat_count):
    feat_rows, model_width = dec_table.shape
    slot_count = 2 * entries_dev // feat_count
    ids_blocks = act_ids.reshape(feat_count, entries_dev)
    owner_ids = ids_blocks // feat_rows
    local_ids = ids_blocks % feat_rows
    owned_mask = owner_ids == feat_index
    entry_iota = jnp.arange(entries_dev, dtype=jnp.int32)
    before = (entry_iota[:, None] < entry_iota[None, :]).astype(BF)
    slot_rank = jnp.dot(owned_mask.astype(BF), before, preferred_element_type=F32).astype(jnp.int32)
    slot_iota = jnp.arange(slot_count, dtype=jnp.int32)
    selected = (
        owned_mask[:, None, :] & (slot_rank[:, None, :] == slot_iota[None, :, None])
    ).astype(jnp.int32)
    source_row = jnp.sum(selected * local_ids[:, None, :], axis=2)
    outgoing = jnp.take(dec_table, source_row.reshape(-1), axis=0).reshape(
        feat_count, slot_count, model_width
    )
    own_owner = lax.dynamic_index_in_dim(owner_ids, feat_index, 0, keepdims=False)
    earlier = (entry_iota[None, :] < entry_iota[:, None]).astype(jnp.int32)
    same_owner = (own_owner[:, None] == own_owner[None, :]).astype(jnp.int32)
    own_rank = jnp.sum(earlier * same_owner, axis=1)
    flat_index = own_owner * slot_count + own_rank
    return outgoing, flat_index


def per_device(
    decoders,
    encoders,
    out_proj,
    value_proj,
    attention,
    norm_scale,
    act_ids,
    act_values,
    target_ids,
    target_pos,
):
    sections = lax.axis_size("section")
    section_index = lax.axis_index("section")
    feat_index = lax.axis_index(FEAT)
    feat_count = lax.axis_size(FEAT)
    model_width = decoders.shape[2]
    half = model_width // 2
    feat_rows = decoders.shape[1]
    seq_len = attention.shape[2]
    head_width = out_proj.shape[1]
    entries_dev = act_values.shape[1]
    targets = target_ids.shape[0]

    own = jnp.concatenate([out_proj[0], value_proj[0].T], axis=0)
    own_mix = attention[0, 0]
    beyond = lax.ppermute(own, "zh", SWAP)
    near = neighbour_heads(own)

    feat_iota = jnp.arange(feat_rows, dtype=jnp.int32)
    target_pick = (
        (target_ids - feat_index * feat_rows)[:, None] == feat_iota[None, :]
    ).astype(BF)
    enc_rows = jnp.dot(target_pick, encoders[0], preferred_element_type=F32).astype(BF)
    enc_send = jnp.broadcast_to(
        enc_rows[None, :, None, :], (QUADS, targets, 2, model_width)
    ).reshape(feat_count, model_width)
    near_mix = neighbour_heads(own_mix)
    zh_mix = lax.ppermute(jnp.stack([own_mix, near_mix]), "zh", SWAP)
    outgoing, flat_index = panel_route(
        decoders[0], act_ids[0], entries_dev, feat_index, feat_count
    )
    own, beyond, near, near_mix, zh_mix, outgoing, enc_send = lax.optimization_barrier(
        (own, beyond, near, near_mix, zh_mix, outgoing, enc_send)
    )
    far = neighbour_heads(beyond)
    enc_got = lax.all_to_all(enc_send, FEAT, split_axis=0, concat_axis=0, tiled=True)
    enc_row = jnp.sum(enc_got.astype(F32), axis=0)
    own_target = lax.axis_index(("par", "zh"))
    own_pos = lax.dynamic_index_in_dim(target_pos, own_target, 0, keepdims=False)
    positions = jnp.arange(seq_len, dtype=jnp.int32)
    start = jnp.where((positions == own_pos)[:, None], enc_row[None, :], 0.0)

    groups = [prepare(head) for head in (own, near, beyond)]
    core_mix = jnp.stack([own_mix, near_mix, zh_mix[0], zh_mix[1]])
    mixing = jnp.stack([core_mix, lax.ppermute(core_mix, "core", SWAP)], axis=1)
    mixing = mixing.reshape(-1, seq_len, seq_len)
    heads = mixing.shape[0]
    mix_wide = jnp.broadcast_to(
        mixing.transpose(1, 2, 0)[..., None], (seq_len, seq_len, heads, head_width)
    ).reshape(seq_len, seq_len, heads * head_width)
    quarter = (start * 0.25).astype(BF)
    far, groups, mix_wide, quarter, outgoing = lax.optimization_barrier(
        (far, groups, mix_wide, quarter, outgoing)
    )
    incoming = lax.all_to_all(outgoing, FEAT, split_axis=0, concat_axis=0, tiled=True)
    panel = jnp.take(incoming.reshape(-1, model_width), flat_index, axis=0)
    groups.append(prepare(far))
    outs = [group[0] for group in groups]
    values = [group[1] for group in groups]
    scales = norm_scale[0][:, None]

    outs, values = [keep(w) for w in outs], [keep(w) for w in values]
    mix_wide = keep(mix_wide)
    core = lax.axis_index("core").reshape(1)
    arrived = (quarter, quarter)
    history = []
    for step in range(sections - 1):
        if step == PANEL_BY:
            arrived, panel = lax.optimization_barrier((arrived, panel))
        part, rounded, grad_part = head_grads(arrived, outs)
        history.append(rounded)
        grads = lax.all_gather(grad_part, "core", axis=0)
        share = head_terms(core, grads, mix_wide, part, scales, values)
        arrived = tuple(send_down(share, turn, sections) for turn in (1, 0))
    history.append((arrived[0].astype(F32) + arrived[1].astype(F32)).astype(BF))

    steps_each = sections // QUADS
    held = jnp.stack(history)
    first = lax.axis_index("y2") * steps_each
    held = lax.dynamic_slice_in_dim(held, first, steps_each, 0).transpose(1, 0, 2)
    this_half = lax.dynamic_slice_in_dim(held, core[0] * half, half, 2)
    other_half = lax.dynamic_slice_in_dim(held, (1 - core[0]) * half, half, 2)
    got_half = lax.ppermute(other_half, "core", SWAP)
    held = (this_half.astype(F32) + got_half.astype(F32)).astype(BF)
    got = lax.all_to_all(held, CHIPS, split_axis=0, concat_axis=0, tiled=True)
    got = lax.all_gather(got.reshape(-1, half), "core", axis=0)
    raw = sum(
        lax.dot_general(
            got[side],
            panel[:, side * half : (side + 1) * half],
            (((1,), (1,)), ((), ())),
            preferred_element_type=F32,
        )
        for side in range(2)
    )
    edges = raw.reshape(QUADS, targets, steps_each, entries_dev).transpose(0, 2, 1, 3)
    edges = edges.reshape(sections * targets, entries_dev) * act_values[0][None, :]
    padded = jnp.concatenate([jnp.zeros_like(edges), edges], axis=0)
    edges = lax.dynamic_slice_in_dim(
        padded, (sections - section_index) * targets, sections * targets, 0
    )
    return edges[None]


def solution(mesh):
    sections = mesh.shape["section"]
    fine = Mesh(mesh.devices.reshape(sections, 4, 2, 2, 2), ("section", *FEAT))
    in_specs = (
        P("section", FEAT, None),
        P("section", FEAT, None),
        P("section", FEAT, None),
        P("section", None, FEAT),
        P("section", FEAT, None, None),
        P("section", None),
        P("section", None),
        P("section", FEAT),
        P("section"),
        P("section"),
    )
    return jax.shard_map(
        per_device, mesh=fine, in_specs=in_specs, out_specs=P("section", None, FEAT), check_vma=False
    )
```

```python
import jax
import jax.numpy as jnp
from jax import lax
from jax.experimental import pallas as pl
from jax.experimental.pallas import tpu as pltpu
from jax.sharding import Mesh, PartitionSpec as P

K_ACT = 256
BF = jnp.bfloat16
F32 = jnp.float32
FEAT = ("y2", "par", "zh", "core")
CHIPS = ("y2", "par", "zh")
QUADS = 4
PANEL_BY = 5
SWAP = [(0, 1), (1, 0)]


def neighbour_heads(shard):
    pairs = []
    for y in range(8):
        pairs.append((2 * y, 2 * ((y - 1) % 8)))
        pairs.append((2 * y + 1, 2 * ((y + 1) % 8) + 1))
    split = [(y * 2 + core) for y in range(8) for core in range(2)]
    assert len(split) == len(pairs)
    return lax.ppermute(shard, ("y2", "par", "core"), pairs)


def send_down(shard, turn, sections):
    places = {0: ((0, 0), (3, 1)), 1: ((2, 1), (1, 0))}[turn]
    pairs = []
    for section in range(1, sections):
        for i in range(QUADS):
            for core, (by, to_core) in enumerate(places):
                below = (section - 1) * QUADS + (i + by) % QUADS
                pairs.append(((section * QUADS + i) * 2 + core, below * 2 + to_core))
    return lax.ppermute(shard, ("section", "y2", "core"), pairs)


def grads_kernel(first_ref, second_ref, *refs):
    *outs, part_ref, rounded_ref, grads_ref = refs
    part = first_ref[...].astype(F32) + second_ref[...].astype(F32)
    part_ref[...] = part
    rounded = part.astype(BF)
    rounded_ref[...] = rounded
    wide = outs[0].shape[1]
    for k, ref in enumerate(outs):
        grads_ref[:, k * wide : (k + 1) * wide] = jnp.dot(
            rounded, ref[...], preferred_element_type=F32
        )


def terms_kernel(core_ref, grads_ref, mix_ref, part_ref, scales_ref, *refs):
    *values, share_ref = refs
    core = core_ref[0]
    mine, other = grads_ref[core], grads_ref[1 - core]
    wide = values[0].shape[0]
    head = wide // 2
    swapped = []
    for k in range(2 * len(values)):
        swapped.append(other[:, (k ^ 1) * head : ((k ^ 1) + 1) * head])
    grads = mine + jnp.concatenate(swapped, axis=1)
    mixed = mix_ref[0] * grads[0:1, :]
    for p in range(1, grads.shape[0]):
        mixed = mixed + mix_ref[p] * grads[p : p + 1, :]
    mixed = mixed.astype(BF)
    term = None
    for k, ref in enumerate(values):
        product = jnp.dot(
            mixed[:, k * wide : (k + 1) * wide],
            ref[...],
            preferred_element_type=F32,
        )
        term = product if term is None else term + product
    share_ref[...] = (part_ref[...] * 0.5 + term * scales_ref[...]).astype(BF)


def turn_kernel(mine_ref, other_ref, turned_ref, values_ref):
    head = mine_ref.shape[0] // 2
    turned_ref[:, :head] = mine_ref[:head, :].T
    turned_ref[:, head:] = other_ref[:head, :].T
    values_ref[:head, :] = mine_ref[head:, :]
    values_ref[head:, :] = other_ref[head:, :]


def keep(array):
    return pltpu.with_memory_space_constraint(array, pltpu.VMEM)


def whole():
    return pl.BlockSpec(memory_space=pltpu.VMEM)


def prepare(mine):
    other = lax.ppermute(mine, "core", SWAP)
    rows, model_width = mine.shape
    return pl.pallas_call(
        turn_kernel,
        out_shape=(
            jax.ShapeDtypeStruct((model_width, rows), BF),
            jax.ShapeDtypeStruct((rows, model_width), BF),
        ),
        in_specs=[whole()] * 2,
        out_specs=(whole(),) * 2,
        compiler_params=pltpu.CompilerParams(vmem_limit_bytes=24 << 20),
        name="turn_heads",
    )(mine, other)


def head_grads(arrived, outs):
    seq_len, model_width = arrived[0].shape
    heads_wide = sum(w.shape[1] for w in outs)
    return pl.pallas_call(
        grads_kernel,
        out_shape=(
            jax.ShapeDtypeStruct((seq_len, model_width), F32),
            jax.ShapeDtypeStruct((seq_len, model_width), BF),
            jax.ShapeDtypeStruct((seq_len, heads_wide), F32),
        ),
        in_specs=[whole()] * (2 + len(outs)),
        out_specs=(whole(),) * 3,
        compiler_params=pltpu.CompilerParams(vmem_limit_bytes=24 << 20),
        name="head_grads",
    )(*arrived, *outs)


def head_terms(core, grads, mix_wide, part, scales, values):
    return pl.pallas_call(
        terms_kernel,
        out_shape=jax.ShapeDtypeStruct(part.shape, BF),
        in_specs=[pl.BlockSpec(memory_space=pltpu.SMEM)] + [whole()] * (4 + len(values)),
        out_specs=whole(),
        compiler_params=pltpu.CompilerParams(vmem_limit_bytes=24 << 20),
        name="head_terms",
    )(core, grads, mix_wide, part, scales, *values)


def panel_route(dec_table, act_ids, entries_dev, feat_index, feat_count):
    feat_rows, model_width = dec_table.shape
    slot_count = 2 * entries_dev // feat_count
    ids_blocks = act_ids.reshape(feat_count, entries_dev)
    owner_ids = ids_blocks // feat_rows
    local_ids = ids_blocks % feat_rows
    owned_mask = owner_ids == feat_index
    entry_iota = jnp.arange(entries_dev, dtype=jnp.int32)
    before = (entry_iota[:, None] < entry_iota[None, :]).astype(BF)
    slot_rank = jnp.dot(owned_mask.astype(BF), before, preferred_element_type=F32).astype(jnp.int32)
    slot_iota = jnp.arange(slot_count, dtype=jnp.int32)
    selected = (
        owned_mask[:, None, :] & (slot_rank[:, None, :] == slot_iota[None, :, None])
    ).astype(jnp.int32)
    source_row = jnp.sum(selected * local_ids[:, None, :], axis=2)
    outgoing = jnp.take(dec_table, source_row.reshape(-1), axis=0).reshape(
        feat_count, slot_count, model_width
    )
    own_owner = lax.dynamic_index_in_dim(owner_ids, feat_index, 0, keepdims=False)
    earlier = (entry_iota[None, :] < entry_iota[:, None]).astype(jnp.int32)
    same_owner = (own_owner[:, None] == own_owner[None, :]).astype(jnp.int32)
    own_rank = jnp.sum(earlier * same_owner, axis=1)
    flat_index = own_owner * slot_count + own_rank
    return outgoing, flat_index


def per_device(
    decoders,
    encoders,
    out_proj,
    value_proj,
    attention,
    norm_scale,
    act_ids,
    act_values,
    target_ids,
    target_pos,
):
    sections = lax.axis_size("section")
    section_index = lax.axis_index("section")
    feat_index = lax.axis_index(FEAT)
    feat_count = lax.axis_size(FEAT)
    model_width = decoders.shape[2]
    half = model_width // 2
    feat_rows = decoders.shape[1]
    seq_len = attention.shape[2]
    head_width = out_proj.shape[1]
    entries_dev = act_values.shape[1]
    targets = target_ids.shape[0]

    own = jnp.concatenate([out_proj[0], value_proj[0].T], axis=0)
    own_mix = attention[0, 0]
    beyond = lax.ppermute(own, "zh", SWAP)

    feat_iota = jnp.arange(feat_rows, dtype=jnp.int32)
    target_pick = (
        (target_ids - feat_index * feat_rows)[:, None] == feat_iota[None, :]
    ).astype(BF)
    enc_rows = jnp.dot(target_pick, encoders[0], preferred_element_type=F32).astype(BF)
    enc_send = jnp.broadcast_to(
        enc_rows[None, :, None, :], (QUADS, targets, 2, model_width)
    ).reshape(feat_count, model_width)
    near_mix = neighbour_heads(own_mix)
    own, near_mix = lax.optimization_barrier((own, near_mix))
    near = neighbour_heads(own)
    zh_mix = lax.ppermute(jnp.stack([own_mix, near_mix]), "zh", SWAP)
    outgoing, flat_index = panel_route(
        decoders[0], act_ids[0], entries_dev, feat_index, feat_count
    )
    beyond, outgoing, near_mix, zh_mix = lax.optimization_barrier(
        (beyond, outgoing, near_mix, zh_mix)
    )
    far = neighbour_heads(beyond)
    enc_got = lax.all_to_all(enc_send, FEAT, split_axis=0, concat_axis=0, tiled=True)
    enc_row = jnp.sum(enc_got.astype(F32), axis=0)
    own_target = lax.axis_index(("par", "zh"))
    own_pos = lax.dynamic_index_in_dim(target_pos, own_target, 0, keepdims=False)
    positions = jnp.arange(seq_len, dtype=jnp.int32)
    start = jnp.where((positions == own_pos)[:, None], enc_row[None, :], 0.0)

    groups = [prepare(head) for head in (own, near, beyond)]
    core_mix = jnp.stack([own_mix, near_mix, zh_mix[0], zh_mix[1]])
    mixing = jnp.stack([core_mix, lax.ppermute(core_mix, "core", SWAP)], axis=1)
    mixing = mixing.reshape(-1, seq_len, seq_len)
    heads = mixing.shape[0]
    mix_wide = jnp.broadcast_to(
        mixing.transpose(1, 2, 0)[..., None], (seq_len, seq_len, heads, head_width)
    ).reshape(seq_len, seq_len, heads * head_width)
    quarter = (start * 0.25).astype(BF)
    far, groups, mix_wide, outgoing = lax.optimization_barrier(
        (far, groups, mix_wide, outgoing)
    )
    incoming = lax.all_to_all(outgoing, FEAT, split_axis=0, concat_axis=0, tiled=True)
    panel = jnp.take(incoming.reshape(-1, model_width), flat_index, axis=0)
    groups.append(prepare(far))
    outs = [group[0] for group in groups]
    values = [group[1] for group in groups]
    scales = norm_scale[0][:, None]

    outs, values = [keep(w) for w in outs], [keep(w) for w in values]
    mix_wide = keep(mix_wide)
    core = lax.axis_index("core").reshape(1)
    arrived = (quarter, quarter)
    history = []
    for step in range(sections - 1):
        if step == PANEL_BY:
            arrived, panel = lax.optimization_barrier((arrived, panel))
        part, rounded, grad_part = head_grads(arrived, outs)
        history.append(rounded)
        grads = lax.all_gather(grad_part, "core", axis=0)
        share = head_terms(core, grads, mix_wide, part, scales, values)
        arrived = tuple(send_down(share, turn, sections) for turn in (1, 0))
    history.append((arrived[0].astype(F32) + arrived[1].astype(F32)).astype(BF))

    steps_each = sections // QUADS
    held = jnp.stack(history)
    first = lax.axis_index("y2") * steps_each
    held = lax.dynamic_slice_in_dim(held, first, steps_each, 0).transpose(1, 0, 2)
    this_half = lax.dynamic_slice_in_dim(held, core[0] * half, half, 2)
    other_half = lax.dynamic_slice_in_dim(held, (1 - core[0]) * half, half, 2)
    got_half = lax.ppermute(other_half, "core", SWAP)
    held = (this_half.astype(F32) + got_half.astype(F32)).astype(BF)
    got = lax.all_to_all(held, CHIPS, split_axis=0, concat_axis=0, tiled=True)
    got = lax.all_gather(got.reshape(-1, half), "core", axis=0)
    raw = sum(
        lax.dot_general(
            got[side],
            panel[:, side * half : (side + 1) * half],
            (((1,), (1,)), ((), ())),
            preferred_element_type=F32,
        )
        for side in range(2)
    )
    edges = raw.reshape(QUADS, targets, steps_each, entries_dev).transpose(0, 2, 1, 3)
    edges = edges.reshape(sections * targets, entries_dev) * act_values[0][None, :]
    padded = jnp.concatenate([jnp.zeros_like(edges), edges], axis=0)
    edges = lax.dynamic_slice_in_dim(
        padded, (sections - section_index) * targets, sections * targets, 0
    )
    return edges[None]


def solution(mesh):
    sections = mesh.shape["section"]
    fine = Mesh(mesh.devices.reshape(sections, 4, 2, 2, 2), ("section", *FEAT))
    in_specs = (
        P("section", FEAT, None),
        P("section", FEAT, None),
        P("section", FEAT, None),
        P("section", None, FEAT),
        P("section", FEAT, None, None),
        P("section", None),
        P("section", None),
        P("section", FEAT),
        P("section"),
        P("section"),
    )
    return jax.shard_map(
        per_device, mesh=fine, in_specs=in_specs, out_specs=P("section", None, FEAT), check_vma=False
    )
```

```python
import jax
import jax.numpy as jnp
from jax import lax
from jax.experimental import pallas as pl
from jax.experimental.pallas import tpu as pltpu
from jax.sharding import Mesh, PartitionSpec as P

K_ACT = 256
BF = jnp.bfloat16
F32 = jnp.float32
FEAT = ("y2", "par", "zh", "core")
CHIPS = ("y2", "par", "zh")
QUADS = 4
PANEL_BY = 5
SWAP = [(0, 1), (1, 0)]


def neighbour_heads(shard):
    pairs = []
    for y in range(8):
        pairs.append((2 * y, 2 * ((y - 1) % 8)))
        pairs.append((2 * y + 1, 2 * ((y + 1) % 8) + 1))
    split = [(y * 2 + core) for y in range(8) for core in range(2)]
    assert len(split) == len(pairs)
    return lax.ppermute(shard, ("y2", "par", "core"), pairs)


def send_down(shard, turn, sections):
    places = {0: ((0, 0), (3, 1)), 1: ((2, 1), (1, 0))}[turn]
    pairs = []
    for section in range(1, sections):
        for i in range(QUADS):
            for core, (by, to_core) in enumerate(places):
                below = (section - 1) * QUADS + (i + by) % QUADS
                pairs.append(((section * QUADS + i) * 2 + core, below * 2 + to_core))
    return lax.ppermute(shard, ("section", "y2", "core"), pairs)


def grads_kernel(first_ref, second_ref, *refs):
    *outs, part_ref, rounded_ref, grads_ref = refs
    part = first_ref[...].astype(F32) + second_ref[...].astype(F32)
    part_ref[...] = part
    rounded = part.astype(BF)
    rounded_ref[...] = rounded
    wide = outs[0].shape[1]
    for k, ref in enumerate(outs):
        grads_ref[:, k * wide : (k + 1) * wide] = jnp.dot(
            rounded, ref[...], preferred_element_type=F32
        )


def terms_kernel(core_ref, grads_ref, mix_ref, part_ref, scales_ref, *refs):
    *values, share_ref = refs
    core = core_ref[0]
    mine, other = grads_ref[core], grads_ref[1 - core]
    wide = values[0].shape[0]
    head = wide // 2
    swapped = []
    for k in range(2 * len(values)):
        swapped.append(other[:, (k ^ 1) * head : ((k ^ 1) + 1) * head])
    grads = mine + jnp.concatenate(swapped, axis=1)
    mixed = mix_ref[0] * grads[0:1, :]
    for p in range(1, grads.shape[0]):
        mixed = mixed + mix_ref[p] * grads[p : p + 1, :]
    mixed = mixed.astype(BF)
    term = None
    for k, ref in enumerate(values):
        product = jnp.dot(
            mixed[:, k * wide : (k + 1) * wide],
            ref[...],
            preferred_element_type=F32,
        )
        term = product if term is None else term + product
    share_ref[...] = (part_ref[...] * 0.5 + term * scales_ref[...]).astype(BF)


def turn_kernel(mine_ref, other_ref, turned_ref, values_ref):
    head = mine_ref.shape[0] // 2
    turned_ref[:, :head] = mine_ref[:head, :].T
    turned_ref[:, head:] = other_ref[:head, :].T
    values_ref[:head, :] = mine_ref[head:, :]
    values_ref[head:, :] = other_ref[head:, :]


def keep(array):
    return pltpu.with_memory_space_constraint(array, pltpu.VMEM)


def whole():
    return pl.BlockSpec(memory_space=pltpu.VMEM)


def prepare(mine):
    other = lax.ppermute(mine, "core", SWAP)
    rows, model_width = mine.shape
    return pl.pallas_call(
        turn_kernel,
        out_shape=(
            jax.ShapeDtypeStruct((model_width, rows), BF),
            jax.ShapeDtypeStruct((rows, model_width), BF),
        ),
        in_specs=[whole()] * 2,
        out_specs=(whole(),) * 2,
        compiler_params=pltpu.CompilerParams(vmem_limit_bytes=24 << 20),
        name="turn_heads",
    )(mine, other)


def head_grads(arrived, outs):
    seq_len, model_width = arrived[0].shape
    heads_wide = sum(w.shape[1] for w in outs)
    return pl.pallas_call(
        grads_kernel,
        out_shape=(
            jax.ShapeDtypeStruct((seq_len, model_width), F32),
            jax.ShapeDtypeStruct((seq_len, model_width), BF),
            jax.ShapeDtypeStruct((seq_len, heads_wide), F32),
        ),
        in_specs=[whole()] * (2 + len(outs)),
        out_specs=(whole(),) * 3,
        compiler_params=pltpu.CompilerParams(vmem_limit_bytes=24 << 20),
        name="head_grads",
    )(*arrived, *outs)


def head_terms(core, grads, mix_wide, part, scales, values):
    return pl.pallas_call(
        terms_kernel,
        out_shape=jax.ShapeDtypeStruct(part.shape, BF),
        in_specs=[pl.BlockSpec(memory_space=pltpu.SMEM)] + [whole()] * (4 + len(values)),
        out_specs=whole(),
        compiler_params=pltpu.CompilerParams(vmem_limit_bytes=24 << 20),
        name="head_terms",
    )(core, grads, mix_wide, part, scales, *values)


def panel_route(dec_table, act_ids, entries_dev, feat_index, feat_count):
    feat_rows, model_width = dec_table.shape
    slot_count = 2 * entries_dev // feat_count
    ids_blocks = act_ids.reshape(feat_count, entries_dev)
    owner_ids = ids_blocks // feat_rows
    local_ids = ids_blocks % feat_rows
    owned_mask = owner_ids == feat_index
    entry_iota = jnp.arange(entries_dev, dtype=jnp.int32)
    before = (entry_iota[:, None] < entry_iota[None, :]).astype(BF)
    slot_rank = jnp.dot(owned_mask.astype(BF), before, preferred_element_type=F32).astype(jnp.int32)
    slot_iota = jnp.arange(slot_count, dtype=jnp.int32)
    selected = (
        owned_mask[:, None, :] & (slot_rank[:, None, :] == slot_iota[None, :, None])
    ).astype(jnp.int32)
    source_row = jnp.sum(selected * local_ids[:, None, :], axis=2)
    outgoing = jnp.take(dec_table, source_row.reshape(-1), axis=0).reshape(
        feat_count, slot_count, model_width
    )
    own_owner = lax.dynamic_index_in_dim(owner_ids, feat_index, 0, keepdims=False)
    earlier = (entry_iota[None, :] < entry_iota[:, None]).astype(jnp.int32)
    same_owner = (own_owner[:, None] == own_owner[None, :]).astype(jnp.int32)
    own_rank = jnp.sum(earlier * same_owner, axis=1)
    flat_index = own_owner * slot_count + own_rank
    return outgoing, flat_index


def per_device(
    decoders,
    encoders,
    out_proj,
    value_proj,
    attention,
    norm_scale,
    act_ids,
    act_values,
    target_ids,
    target_pos,
):
    sections = lax.axis_size("section")
    section_index = lax.axis_index("section")
    feat_index = lax.axis_index(FEAT)
    feat_count = lax.axis_size(FEAT)
    model_width = decoders.shape[2]
    half = model_width // 2
    feat_rows = decoders.shape[1]
    seq_len = attention.shape[2]
    head_width = out_proj.shape[1]
    entries_dev = act_values.shape[1]
    targets = target_ids.shape[0]

    own = jnp.concatenate([out_proj[0], value_proj[0].T], axis=0)
    own_mix = attention[0, 0]
    beyond = lax.ppermute(own, "zh", SWAP)

    feat_iota = jnp.arange(feat_rows, dtype=jnp.int32)
    target_pick = (
        (target_ids - feat_index * feat_rows)[:, None] == feat_iota[None, :]
    ).astype(BF)
    enc_rows = jnp.dot(target_pick, encoders[0], preferred_element_type=F32).astype(BF)
    enc_send = jnp.broadcast_to(
        enc_rows[None, :, None, :], (QUADS, targets, 2, model_width)
    ).reshape(feat_count, model_width)
    near_mix = neighbour_heads(own_mix)
    own, near_mix, enc_send = lax.optimization_barrier((own, near_mix, enc_send))
    near = neighbour_heads(own)
    zh_mix = lax.ppermute(jnp.stack([own_mix, near_mix]), "zh", SWAP)
    outgoing, flat_index = panel_route(
        decoders[0], act_ids[0], entries_dev, feat_index, feat_count
    )
    enc_got = lax.all_to_all(enc_send, FEAT, split_axis=0, concat_axis=0, tiled=True)
    beyond, outgoing, near_mix, zh_mix, enc_got = lax.optimization_barrier(
        (beyond, outgoing, near_mix, zh_mix, enc_got)
    )
    far = neighbour_heads(beyond)
    incoming = lax.all_to_all(outgoing, FEAT, split_axis=0, concat_axis=0, tiled=True)
    enc_row = jnp.sum(enc_got.astype(F32), axis=0)
    own_target = lax.axis_index(("par", "zh"))
    own_pos = lax.dynamic_index_in_dim(target_pos, own_target, 0, keepdims=False)
    positions = jnp.arange(seq_len, dtype=jnp.int32)
    start = jnp.where((positions == own_pos)[:, None], enc_row[None, :], 0.0)

    groups = [prepare(head) for head in (own, near, beyond)]
    core_mix = jnp.stack([own_mix, near_mix, zh_mix[0], zh_mix[1]])
    mixing = jnp.stack([core_mix, lax.ppermute(core_mix, "core", SWAP)], axis=1)
    mixing = mixing.reshape(-1, seq_len, seq_len)
    heads = mixing.shape[0]
    mix_wide = jnp.broadcast_to(
        mixing.transpose(1, 2, 0)[..., None], (seq_len, seq_len, heads, head_width)
    ).reshape(seq_len, seq_len, heads * head_width)
    quarter = (start * 0.25).astype(BF)
    far, groups, mix_wide = lax.optimization_barrier((far, groups, mix_wide))
    panel = jnp.take(incoming.reshape(-1, model_width), flat_index, axis=0)
    groups.append(prepare(far))
    outs = [group[0] for group in groups]
    values = [group[1] for group in groups]
    scales = norm_scale[0][:, None]

    outs, values = [keep(w) for w in outs], [keep(w) for w in values]
    mix_wide = keep(mix_wide)
    core = lax.axis_index("core").reshape(1)
    arrived = (quarter, quarter)
    history = []
    for step in range(sections - 1):
        if step == PANEL_BY:
            arrived, panel = lax.optimization_barrier((arrived, panel))
        part, rounded, grad_part = head_grads(arrived, outs)
        history.append(rounded)
        grads = lax.all_gather(grad_part, "core", axis=0)
        share = head_terms(core, grads, mix_wide, part, scales, values)
        arrived = tuple(send_down(share, turn, sections) for turn in (1, 0))
    history.append((arrived[0].astype(F32) + arrived[1].astype(F32)).astype(BF))

    steps_each = sections // QUADS
    held = jnp.stack(history)
    first = lax.axis_index("y2") * steps_each
    held = lax.dynamic_slice_in_dim(held, first, steps_each, 0).transpose(1, 0, 2)
    this_half = lax.dynamic_slice_in_dim(held, core[0] * half, half, 2)
    other_half = lax.dynamic_slice_in_dim(held, (1 - core[0]) * half, half, 2)
    got_half = lax.ppermute(other_half, "core", SWAP)
    held = (this_half.astype(F32) + got_half.astype(F32)).astype(BF)
    got = lax.all_to_all(held, CHIPS, split_axis=0, concat_axis=0, tiled=True)
    got = lax.all_gather(got.reshape(-1, half), "core", axis=0)
    raw = sum(
        lax.dot_general(
            got[side],
            panel[:, side * half : (side + 1) * half],
            (((1,), (1,)), ((), ())),
            preferred_element_type=F32,
        )
        for side in range(2)
    )
    edges = raw.reshape(QUADS, targets, steps_each, entries_dev).transpose(0, 2, 1, 3)
    edges = edges.reshape(sections * targets, entries_dev) * act_values[0][None, :]
    padded = jnp.concatenate([jnp.zeros_like(edges), edges], axis=0)
    edges = lax.dynamic_slice_in_dim(
        padded, (sections - section_index) * targets, sections * targets, 0
    )
    return edges[None]


def solution(mesh):
    sections = mesh.shape["section"]
    fine = Mesh(mesh.devices.reshape(sections, 4, 2, 2, 2), ("section", *FEAT))
    in_specs = (
        P("section", FEAT, None),
        P("section", FEAT, None),
        P("section", FEAT, None),
        P("section", None, FEAT),
        P("section", FEAT, None, None),
        P("section", None),
        P("section", None),
        P("section", FEAT),
        P("section"),
        P("section"),
    )
    return jax.shard_map(
        per_device, mesh=fine, in_specs=in_specs, out_specs=P("section", None, FEAT), check_vma=False
    )
```
